32 devices in a mesh: grp: 2 (over x), aa: 16 (over z, y, core).
Axes of the slice: x: 2, y: 2, z: 4, core: 2. Of those that a mesh axis runs over, the one named last changes fastest.
Arguments:
- amplitudes: float32 [96, 128, 128], P('aa', 'grp'), parts along dimension 1, may hold values from -6 to 6
- integrals: float32 [6144, 16, 128], P(('grp', 'aa')), parts along dimension 0, may hold values from -0.125 to 0.125
- irrep_sizes: int32 [8], replicated, may hold values from 1 to 16, 96 in all
- home: int32 [96], replicated, may hold values from 0 to 95, as said below
- row_irrep: int32 [16], replicated, may hold values from 0 to 7
Outputs:
- residual: float32 [128, 3072], P('grp', 'aa'), parts along dimension 0
The draws below stay inside these ranges and needn't reach their ends.
There are 2 independent parts, one for each index of `grp`. The reference program is written for one: setup_inputs(seed, part) draws one part's arguments, and reference() takes and returns one part's arrays. A program takes and returns all parts, laid end to end along the dimension named above; an argument that names none is the same for every part. Nothing has to cross between parts.
Inputs may be any that keep to these rules, and one draw needn't show every extreme that they name: `home`: a permutation of 0 .. 95; the positions of one irrep map to rows on distinct indices of aa (row // 6).
All inputs are finite; a program needn't handle non-finite values.
Results may differ from the reference program's by a relative error of at most 0.0003.
Values sent between devices are 32-bit elements; how exact they have to be, the bound alone decides.
A program may use at most 192 MiB of HBM per device.

```python
import math
import jax
import jax.numpy as jnp
import numpy as np
from jax import lax

PAIRS = 64
CB = 128
ROWB = 192
CB_DEV = 6
IRREPS = 8
IRR_MOST = 16
NCB = 96
ROWS = 3072
N_AA = 16


def draw_home(key, part):
    key = jax.random.fold_in(key, 5)
    shuffle = jax.random.permutation(key, N_AA).astype(jnp.int32)
    position = jnp.arange(NCB, dtype=jnp.int32)
    return (shuffle[position % N_AA] * CB_DEV + position // N_AA).astype(jnp.int32)


def place_ends(values, rng, smallest, top_value):
    longest = values.shape.index(max(values.shape))
    spots = []
    for shift in (0, 1):
        where = [jax.random.randint(jax.random.fold_in(rng, axis), (), 0, length) for axis, length in enumerate(values.shape)]
        where[longest] = (where[longest] + shift) % values.shape[longest]
        spots.append(tuple(where))
    return values.at[spots[0]].set(smallest).at[spots[1]].set(top_value)


def shard_levels(stream_key, extent, split, least, high):
    loudness, own = 1.0, jax.random.fold_in(stream_key, 6)
    for axis_at, blocks in split:
        draws = jnp.exp(jax.random.uniform(jax.random.fold_in(own, axis_at), (blocks,), jnp.float32, least / len(split), high / len(split)))
        loudness = loudness * jnp.repeat(draws, extent[axis_at] // blocks).reshape([-1 if axis == axis_at else 1 for axis in range(len(extent))])
    return loudness


def length_profile(amount, total, most, skew):
    loads = [(1 << 20) // math.isqrt(grade ** skew) + 1 for grade in range(2, amount + 1)]
    spare, counts = total - most - (amount - 1), [1] * (amount - 1)
    while spare > 0:
        movable = [i for i in range(amount - 1) if counts[i] < most]
        pool, left = sum([loads[i] for i in movable]), spare
        for i in movable:
            addition = min(most - counts[i], max(1, left * loads[i] // pool), spare)
            counts[i] = counts[i] + addition
            spare = spare - addition
    return np.array([most] + counts)


def ragged(rng, count, total, bound, skew):
    if count == 2:
        one = jax.random.randint(rng, (), max(1, total - bound), min(bound, total - 1) + 1)
        return jnp.stack([one, total - one])
    sizes = jnp.asarray(length_profile(count, total, bound, skew), jnp.int32)
    pairs = (count - 1) // 2
    donor, sink = sizes[1:1 + 2 * pairs:2], sizes[2:2 + 2 * pairs:2]
    margin = jnp.minimum(donor - 1, bound - sink)
    passed = jax.random.randint(jax.random.fold_in(rng, 1), (pairs,), 0, 1 << 20) % (margin + 1)
    sizes = sizes.at[1:1 + 2 * pairs:2].set(donor - passed).at[2:2 + 2 * pairs:2].set(sink + passed)
    return sizes[jax.random.permutation(jax.random.fold_in(rng, 2), count)]


def scatter_about(stream_key, shape, spread, reach, pieces=(), kind=jnp.bfloat16):
    factor_of = shard_levels(stream_key, shape, pieces, -0.22, 0.18) if pieces else 1.0
    values = jax.random.normal(stream_key, shape, jnp.float32) * spread * factor_of
    return jnp.minimum(jnp.maximum(values, -reach), reach).astype(kind)


def setup_inputs(seed: int = 0, part: int = 0) -> dict:
    key_list = jax.random.split(jax.random.key(seed), 6)
    own_keys = jax.random.split(jax.random.fold_in(key_list[5], part), 6)
    return {
        "amplitudes": scatter_about(own_keys[0], (NCB, PAIRS, CB), 1.0, 6.0, ((0, 16),), jnp.float32),
        "integrals": scatter_about(own_keys[1], (ROWS, IRR_MOST, CB), (IRR_MOST * CB) ** -0.5, 0.125, ((0, 16),), jnp.float32),
        "irrep_sizes": ragged(key_list[2], IRREPS, NCB, IRR_MOST, 1).astype(jnp.int32),
        "home": draw_home(jax.random.fold_in(key_list[5], 71), part),
        "row_irrep": place_ends(jax.random.randint(key_list[4], (N_AA,), 0, IRREPS), jax.random.fold_in(key_list[4], 1), 0, IRREPS - 1).astype(jnp.int32),
    }


def reference(amplitudes, integrals, irrep_sizes, home, row_irrep):
    offsets = (jnp.cumsum(irrep_sizes) - irrep_sizes).astype(jnp.int32)
    slots = jnp.arange(IRR_MOST, dtype=jnp.int32)
    labels = jnp.arange(IRREPS, dtype=jnp.int32)

    def one_owner(owner):
        irrep = row_irrep[owner]
        start_pos = jnp.sum(jnp.where(labels == irrep, offsets, 0)).astype(jnp.int32)
        count = jnp.sum(jnp.where(labels == irrep, irrep_sizes, 0)).astype(jnp.int32)
        positions = jnp.clip(start_pos + slots, 0, NCB - 1).astype(jnp.int32)
        alive = (slots < count).astype(jnp.float32)
        chosen = amplitudes[home[positions]] * alive[:, None, None]
        block = lax.dynamic_slice_in_dim(integrals, (owner * ROWB).astype(jnp.int32), ROWB, 0)
        return 0.5 * jnp.einsum("mpc,rmc->pr", chosen, block, precision=lax.Precision.HIGHEST)

    result = lax.map(one_owner, jnp.arange(N_AA, dtype=jnp.int32))
    return jnp.transpose(result, (1, 0, 2)).reshape(PAIRS, N_AA * ROWB)
```

```python
import functools

import jax
import jax.numpy as jnp
from jax import lax
from jax.experimental import pallas as pl
from jax.experimental.pallas import tpu as pltpu
from jax.sharding import PartitionSpec as P

MESH = pl.DeviceIdType.MESH
UNROLL = 16


def each(first, last, step):
    if last - first <= UNROLL:
        for i in range(first, last):
            step(i)
    else:
        lax.fori_loop(first, last, lambda i, _: (step(i), 0)[1], 0)


def flipped(me, k, n):
    out, bit = me, 1
    while bit < n:
        mine = lax.rem(lax.div(me, bit), 2)
        flip = (k // bit) % 2
        out = out + flip * bit * (1 - 2 * mine)
        bit *= 2
    return out


def scan(count, step, init):
    chunk = 8 if count % 8 == 0 else 1

    def some(outer, state):
        for inner in range(chunk):
            state = step(outer * chunk + inner, state)
        return state

    return lax.fori_loop(0, count // chunk, some, init)


def kernel(n, most, sizes, home, row_irrep, amp, integ, out,
           amp_v, integ_v, send, recv, high, low, slot_of,
           amp_sem, integ_sem, send_sem, recv_sem):
    me = lax.axis_index("aa")
    per = amp.shape[0]
    irreps, total = sizes.shape[0], home.shape[0]
    rows = high.shape[1]

    barrier = pltpu.get_barrier_semaphore()
    each(1, n, lambda k: pl.semaphore_signal(
        barrier, inc=1, device_id={"aa": flipped(me, k, n)}, device_id_type=MESH))
    get_amp = pltpu.make_async_copy(amp, amp_v, amp_sem)
    get_amp.start()
    get_integ = pltpu.make_async_copy(integ, integ_v, integ_sem)
    get_integ.start()

    offsets, at = [], jnp.int32(0)
    for g in range(irreps):
        offsets.append(at)
        at = at + sizes[g]

    def look(i, found):
        which = home[i] - me * per
        return tuple(jnp.where(which == q, i, found[q]) for q in range(per))

    places = scan(total, look, tuple(jnp.int32(0) for _ in range(per)))
    kinds = [sum((p >= offsets[g]).astype(jnp.int32) for g in range(1, irreps)) for p in places]

    get_amp.wait()

    def stage(k):
        dest = flipped(me, k, n)
        wanted = row_irrep[dest]
        pick = jnp.int32(0)
        has = jnp.bool_(False)
        for q in range(per):
            pick = jnp.where(kinds[q] == wanted, q, pick)
            has = has | (kinds[q] == wanted)
        block = amp_v[pick]
        send[dest] = jnp.where(has, block, 0.0)

    each(0, n, stage)

    def hop(k):
        peer = flipped(me, k, n)
        return pltpu.make_async_remote_copy(
            src_ref=send.at[peer], dst_ref=recv.at[me],
            send_sem=send_sem.at[peer], recv_sem=recv_sem.at[me],
            device_id={"aa": peer}, device_id_type=MESH)

    def landing(peer):
        return pltpu.make_async_remote_copy(
            src_ref=send.at[peer], dst_ref=recv.at[peer],
            send_sem=send_sem.at[peer], recv_sem=recv_sem.at[peer],
            device_id={"aa": peer}, device_id_type=MESH)

    pl.semaphore_wait(barrier, n - 1)
    each(0, n - 1, lambda i: hop(n - 1 - i).start())

    mine = row_irrep[me]
    start = jnp.int32(0)
    count = jnp.int32(0)
    for g in range(irreps):
        start = jnp.where(mine == g, offsets[g], start)
        count = jnp.where(mine == g, sizes[g], count)

    def find(source):
        def look_at(m, found):
            row = home[jnp.minimum(start + m, total - 1)] - source * per
            return jnp.where((row >= 0) & (row < per) & (m < count), m, found)

        slot_of[source] = scan(most, look_at, jnp.int32(0))

    each(0, n, find)

    get_integ.wait()

    def split(m):
        full = integ_v[pl.ds(m, rows, stride=most), :]
        top = full.astype(jnp.bfloat16)
        high[m] = top
        low[m] = (full - top.astype(jnp.float32)).astype(jnp.bfloat16)

    each(0, most, split)

    contract = (((1,), (1,)), ((), ()))

    def times(blocks, sources):
        full = jnp.concatenate(blocks, axis=1)
        top = full.astype(jnp.bfloat16)
        rest = (full - top.astype(jnp.float32)).astype(jnp.bfloat16)
        slots = [slot_of[s] for s in sources]
        upper = jnp.concatenate([high[m] for m in slots], axis=1)
        lower = jnp.concatenate([low[m] for m in slots], axis=1)
        both = lax.dot_general(jnp.concatenate([top, rest], axis=0), upper, contract,
                               preferred_element_type=jnp.float32)
        small = lax.dot_general(top, lower, contract, preferred_element_type=jnp.float32)
        half = top.shape[0]
        return both[:half] + (both[half:] + small)

    twin = flipped(me, 1, n)
    landing(twin).wait_recv()
    out[...] = times([send[me], recv[twin]], [me, twin])

    def pair(i):
        one, two = flipped(me, 2 * i, n), flipped(me, 2 * i + 1, n)
        landing(one).wait_recv()
        landing(two).wait_recv()
        out[...] += times([recv[one], recv[two]], [one, two])

    each(1, n // 2, pair)
    out[...] = 0.5 * out[...]
    each(1, n, lambda k: hop(k).wait_send())


def solution(mesh):
    n = mesh.shape["aa"]

    def body(amplitudes, integrals, irrep_sizes, home, row_irrep):
        per, pairs, width = amplitudes.shape
        rows, most, _ = integrals.shape
        smem = pl.BlockSpec(memory_space=pltpu.SMEM)
        hbm = pl.BlockSpec(memory_space=pl.ANY)
        return pl.pallas_call(
            functools.partial(kernel, n, most),
            out_shape=jax.ShapeDtypeStruct((pairs, rows), jnp.float32),
            in_specs=[smem, smem, smem, hbm, hbm],
            out_specs=pl.BlockSpec(memory_space=pltpu.VMEM),
            scratch_shapes=[
                pltpu.VMEM((per, pairs, width), jnp.float32),
                pltpu.VMEM((rows * most, width), jnp.float32),
                pltpu.VMEM((n, pairs, width), jnp.float32),
                pltpu.VMEM((n, pairs, width), jnp.float32),
                pltpu.VMEM((most, rows, width), jnp.bfloat16),
                pltpu.VMEM((most, rows, width), jnp.bfloat16),
                pltpu.SMEM((n,), jnp.int32),
                pltpu.SemaphoreType.DMA,
                pltpu.SemaphoreType.DMA,
                pltpu.SemaphoreType.DMA((n,)),
                pltpu.SemaphoreType.DMA((n,)),
            ],
            compiler_params=pltpu.CompilerParams(
                collective_id=0, has_side_effects=True, vmem_limit_bytes=56 << 20),
        )(irrep_sizes, home, row_irrep, amplitudes, integrals.reshape(rows * most, width))

    return jax.shard_map(
        body,
        mesh=mesh,
        in_specs=(P("aa", "grp", None), P(("grp", "aa"), None, None), P(), P(), P()),
        out_specs=P("grp", "aa"),
        check_vma=False,
    )
```

```python
import functools

import jax
import jax.numpy as jnp
from jax import lax
from jax.experimental import pallas as pl
from jax.experimental.pallas import tpu as pltpu
from jax.sharding import PartitionSpec as P

MESH = pl.DeviceIdType.MESH
UNROLL = 16


def each(first, last, step):
    if last - first <= UNROLL:
        for i in range(first, last):
            step(i)
    else:
        lax.fori_loop(first, last, lambda i, _: (step(i), 0)[1], 0)


def flipped(me, k, n):
    out, bit = me, 1
    while bit < n:
        mine = lax.rem(lax.div(me, bit), 2)
        flip = (k // bit) % 2
        out = out + flip * bit * (1 - 2 * mine)
        bit *= 2
    return out


def scan(count, step, init):
    chunk = 8 if count % 8 == 0 else 1

    def some(outer, state):
        for inner in range(chunk):
            state = step(outer * chunk + inner, state)
        return state

    return lax.fori_loop(0, count // chunk, some, init)


def kernel(n, most, sizes_in, home_in, row_irrep_in, amp, integ, out,
           sizes, home, row_irrep,
           amp_v, integ_v, send, recv, high, low, slot_of,
           index_sem, amp_sem, integ_sem, send_sem, recv_sem):
    me = lax.axis_index("aa")
    per = amp.shape[0]
    irreps, total = sizes.shape[0], home.shape[0]
    rows = high.shape[1]

    barrier = pltpu.get_barrier_semaphore()
    each(1, n, lambda k: pl.semaphore_signal(
        barrier, inc=1, device_id={"aa": flipped(me, k, n)}, device_id_type=MESH))
    get_index = [pltpu.make_async_copy(source, dest, index_sem.at[i]) for i, (source, dest) in enumerate(
        ((home_in, home), (sizes_in, sizes), (row_irrep_in, row_irrep)))]
    for copy in get_index:
        copy.start()
    get_amp = pltpu.make_async_copy(amp, amp_v, amp_sem)
    get_amp.start()
    get_integ = pltpu.make_async_copy(integ, integ_v, integ_sem)
    get_integ.start()

    for copy in get_index:
        copy.wait()
    offsets, at = [], jnp.int32(0)
    for g in range(irreps):
        offsets.append(at)
        at = at + sizes[g]

    def look(i, found):
        which = home[i] - me * per
        return tuple(jnp.where(which == q, i, found[q]) for q in range(per))

    places = scan(total, look, tuple(jnp.int32(0) for _ in range(per)))
    kinds = [sum((p >= offsets[g]).astype(jnp.int32) for g in range(1, irreps)) for p in places]

    get_amp.wait()

    def stage(k):
        dest = flipped(me, k, n)
        wanted = row_irrep[dest]
        pick = jnp.int32(0)
        has = jnp.bool_(False)
        for q in range(per):
            pick = jnp.where(kinds[q] == wanted, q, pick)
            has = has | (kinds[q] == wanted)
        block = amp_v[pick]
        send[dest] = jnp.where(has, block, 0.0)

    each(0, n, stage)

    def hop(k):
        peer = flipped(me, k, n)
        return pltpu.make_async_remote_copy(
            src_ref=send.at[peer], dst_ref=recv.at[me],
            send_sem=send_sem.at[peer], recv_sem=recv_sem.at[me],
            device_id={"aa": peer}, device_id_type=MESH)

    def landing(peer):
        return pltpu.make_async_remote_copy(
            src_ref=send.at[peer], dst_ref=recv.at[peer],
            send_sem=send_sem.at[peer], recv_sem=recv_sem.at[peer],
            device_id={"aa": peer}, device_id_type=MESH)

    pl.semaphore_wait(barrier, n - 1)
    each(0, n - 1, lambda i: hop(i + 1).start())

    mine = row_irrep[me]
    start = jnp.int32(0)
    count = jnp.int32(0)
    for g in range(irreps):
        start = jnp.where(mine == g, offsets[g], start)
        count = jnp.where(mine == g, sizes[g], count)

    def find(source):
        def look_at(m, found):
            row = home[jnp.minimum(start + m, total - 1)] - source * per
            return jnp.where((row >= 0) & (row < per) & (m < count), m, found)

        slot_of[source] = scan(most, look_at, jnp.int32(0))

    each(0, n, find)

    get_integ.wait()

    def split(m):
        full = integ_v[pl.ds(m, rows, stride=most), :]
        top = full.astype(jnp.bfloat16)
        high[m] = top
        low[m] = (full - top.astype(jnp.float32)).astype(jnp.bfloat16)

    each(0, most, split)

    contract = (((1,), (1,)), ((), ()))

    def times(blocks, sources):
        full = jnp.concatenate(blocks, axis=1)
        top = full.astype(jnp.bfloat16)
        rest = (full - top.astype(jnp.float32)).astype(jnp.bfloat16)
        slots = [slot_of[s] for s in sources]
        upper = jnp.concatenate([high[m] for m in slots], axis=1)
        lower = jnp.concatenate([low[m] for m in slots], axis=1)
        both = lax.dot_general(jnp.concatenate([top, rest], axis=0), upper, contract,
                               preferred_element_type=jnp.float32)
        small = lax.dot_general(top, lower, contract, preferred_element_type=jnp.float32)
        half = top.shape[0]
        return both[:half] + (both[half:] + small)

    twin = flipped(me, 1, n)
    landing(twin).wait_recv()
    out[...] = times([send[me], recv[twin]], [me, twin])

    def pair(i):
        one, two = flipped(me, 2 * i, n), flipped(me, 2 * i + 1, n)
        landing(one).wait_recv()
        landing(two).wait_recv()
        out[...] += times([recv[one], recv[two]], [one, two])

    each(1, n // 2, pair)
    out[...] = 0.5 * out[...]
    each(1, n, lambda k: hop(k).wait_send())


def solution(mesh):
    n = mesh.shape["aa"]

    def body(amplitudes, integrals, irrep_sizes, home, row_irrep):
        per, pairs, width = amplitudes.shape
        rows, most, _ = integrals.shape
        hbm = pl.BlockSpec(memory_space=pltpu.HBM)
        return pl.pallas_call(
            functools.partial(kernel, n, most),
            out_shape=pltpu.VMEM((pairs, rows), jnp.float32),
            in_specs=[hbm] * 5,
            out_specs=pl.BlockSpec(memory_space=pltpu.VMEM),
            scratch_shapes=[
                pltpu.SMEM(irrep_sizes.shape, jnp.int32),
                pltpu.SMEM(home.shape, jnp.int32),
                pltpu.SMEM(row_irrep.shape, jnp.int32),
                pltpu.VMEM((per, pairs, width), jnp.float32),
                pltpu.VMEM((rows * most, width), jnp.float32),
                pltpu.VMEM((n, pairs, width), jnp.float32),
                pltpu.VMEM((n, pairs, width), jnp.float32),
                pltpu.VMEM((most, rows, width), jnp.bfloat16),
                pltpu.VMEM((most, rows, width), jnp.bfloat16),
                pltpu.SMEM((n,), jnp.int32),
                pltpu.SemaphoreType.DMA((3,)),
                pltpu.SemaphoreType.DMA,
                pltpu.SemaphoreType.DMA,
                pltpu.SemaphoreType.DMA((n,)),
                pltpu.SemaphoreType.DMA((n,)),
            ],
            compiler_params=pltpu.CompilerParams(
                collective_id=0, has_side_effects=True, vmem_limit_bytes=56 << 20),
        )(irrep_sizes, home, row_irrep, amplitudes, integrals.reshape(rows * most, width))

    return jax.shard_map(
        body,
        mesh=mesh,
        in_specs=(P("aa", "grp", None), P(("grp", "aa"), None, None), P(), P(), P()),
        out_specs=P("grp", "aa"),
        check_vma=False,
    )
```

```python
import functools

import jax
import jax.numpy as jnp
from jax import lax
from jax.experimental import pallas as pl
from jax.experimental.pallas import tpu as pltpu
from jax.sharding import PartitionSpec as P

MESH = pl.DeviceIdType.MESH
UNROLL = 16


def each(first, last, step):
    if last - first <= UNROLL:
        for i in range(first, last):
            step(i)
    else:
        lax.fori_loop(first, last, lambda i, _: (step(i), 0)[1], 0)


def flipped(me, k, n):
    out, bit = me, 1
    while bit < n:
        mine = lax.rem(lax.div(me, bit), 2)
        flip = (k // bit) % 2
        out = out + flip * bit * (1 - 2 * mine)
        bit *= 2
    return out


def scan(count, step, init):
    chunk = 8 if count % 8 == 0 else 1

    def some(outer, state):
        for inner in range(chunk):
            state = step(outer * chunk + inner, state)
        return state

    return lax.fori_loop(0, count // chunk, some, init)


def kernel(n, most, sizes_in, home_in, row_irrep_in, amp, integ, out,
           sizes, home, row_irrep,
           amp_v, integ_v, send, recv, high, low, slot_of,
           index_sem, amp_sem, integ_sem, send_sem, recv_sem):
    me = lax.axis_index("aa")
    per = amp.shape[0]
    irreps, total = sizes.shape[0], home.shape[0]
    rows = high.shape[1]

    barrier = pltpu.get_barrier_semaphore()
    each(1, n, lambda k: pl.semaphore_signal(
        barrier, inc=1, device_id={"aa": flipped(me, k, n)}, device_id_type=MESH))
    get_index = [pltpu.make_async_copy(source, dest, index_sem.at[i]) for i, (source, dest) in enumerate(
        ((home_in, home), (sizes_in, sizes), (row_irrep_in, row_irrep)))]
    for copy in get_index:
        copy.start()
    get_amp = pltpu.make_async_copy(amp, amp_v, amp_sem)
    get_amp.start()
    get_integ = pltpu.make_async_copy(integ, integ_v, integ_sem)
    get_integ.start()

    for copy in get_index:
        copy.wait()
    offsets, at = [], jnp.int32(0)
    for g in range(irreps):
        offsets.append(at)
        at = at + sizes[g]

    def look(i, found):
        which = home[i] - me * per
        return tuple(jnp.where(which == q, i, found[q]) for q in range(per))

    places = scan(total, look, tuple(jnp.int32(0) for _ in range(per)))
    kinds = [sum((p >= offsets[g]).astype(jnp.int32) for g in range(1, irreps)) for p in places]

    get_amp.wait()

    def stage(k):
        dest = flipped(me, k, n)
        wanted = row_irrep[dest]
        pick = jnp.int32(0)
        has = jnp.bool_(False)
        for q in range(per):
            pick = jnp.where(kinds[q] == wanted, q, pick)
            has = has | (kinds[q] == wanted)
        block = amp_v[pick]
        send[dest] = jnp.where(has, block, 0.0)

    each(0, n, stage)

    def hop(k):
        peer = flipped(me, k, n)
        return pltpu.make_async_remote_copy(
            src_ref=send.at[peer], dst_ref=recv.at[me],
            send_sem=send_sem.at[peer], recv_sem=recv_sem.at[me],
            device_id={"aa": peer}, device_id_type=MESH)

    def landing(peer):
        return pltpu.make_async_remote_copy(
            src_ref=send.at[peer], dst_ref=recv.at[peer],
            send_sem=send_sem.at[peer], recv_sem=recv_sem.at[peer],
            device_id={"aa": peer}, device_id_type=MESH)

    pl.semaphore_wait(barrier, n - 1)
    each(0, n - 1, lambda i: hop(i + 1).start())

    mine = row_irrep[me]
    start = jnp.int32(0)
    count = jnp.int32(0)
    for g in range(irreps):
        start = jnp.where(mine == g, offsets[g], start)
        count = jnp.where(mine == g, sizes[g], count)

    def find(source):
        def look_at(m, found):
            row = home[jnp.minimum(start + m, total - 1)] - source * per
            return jnp.where((row >= 0) & (row < per) & (m < count), m, found)

        slot_of[source] = scan(most, look_at, jnp.int32(0))

    each(0, n, find)

    get_integ.wait()

    def split(m):
        full = integ_v[:, m, :]
        top = full.astype(jnp.bfloat16)
        high[m] = top
        low[m] = (full - top.astype(jnp.float32)).astype(jnp.bfloat16)

    each(0, most, split)

    contract = (((1,), (1,)), ((), ()))

    def times(blocks, sources):
        full = jnp.concatenate(blocks, axis=1)
        top = full.astype(jnp.bfloat16)
        rest = (full - top.astype(jnp.float32)).astype(jnp.bfloat16)
        slots = [slot_of[s] for s in sources]
        upper = jnp.concatenate([high[m] for m in slots], axis=1)
        lower = jnp.concatenate([low[m] for m in slots], axis=1)
        both = lax.dot_general(jnp.concatenate([top, rest], axis=0), upper, contract,
                               preferred_element_type=jnp.float32)
        small = lax.dot_general(top, lower, contract, preferred_element_type=jnp.float32)
        half = top.shape[0]
        return both[:half] + (both[half:] + small)

    twin = flipped(me, 1, n)
    landing(twin).wait_recv()
    out[...] = times([send[me], recv[twin]], [me, twin])

    def pair(i):
        one, two = flipped(me, 2 * i, n), flipped(me, 2 * i + 1, n)
        landing(one).wait_recv()
        landing(two).wait_recv()
        out[...] += times([recv[one], recv[two]], [one, two])

    each(1, n // 2 - 1, pair)
    one, two = flipped(me, n - 2, n), flipped(me, n - 1, n)
    landing(one).wait_recv()
    landing(two).wait_recv()
    out[...] = 0.5 * (out[...] + times([recv[one], recv[two]], [one, two]))
    each(1, n, lambda k: hop(k).wait_send())


def solution(mesh):
    n = mesh.shape["aa"]

    def body(amplitudes, integrals, irrep_sizes, home, row_irrep):
        per, pairs, width = amplitudes.shape
        rows, most, _ = integrals.shape
        hbm = pl.BlockSpec(memory_space=pltpu.HBM)
        return pl.pallas_call(
            functools.partial(kernel, n, most),
            out_shape=pltpu.VMEM((pairs, rows), jnp.float32),
            in_specs=[hbm] * 5,
            out_specs=pl.BlockSpec(memory_space=pltpu.VMEM),
            scratch_shapes=[
                pltpu.SMEM(irrep_sizes.shape, jnp.int32),
                pltpu.SMEM(home.shape, jnp.int32),
                pltpu.SMEM(row_irrep.shape, jnp.int32),
                pltpu.VMEM((per, pairs, width), jnp.float32),
                pltpu.VMEM(integrals.shape, jnp.float32),
                pltpu.VMEM((n, pairs, width), jnp.float32),
                pltpu.VMEM((n, pairs, width), jnp.float32),
                pltpu.VMEM((most, rows, width), jnp.bfloat16),
                pltpu.VMEM((most, rows, width), jnp.bfloat16),
                pltpu.SMEM((n,), jnp.int32),
                pltpu.SemaphoreType.DMA((3,)),
                pltpu.SemaphoreType.DMA,
                pltpu.SemaphoreType.DMA,
                pltpu.SemaphoreType.DMA((n,)),
                pltpu.SemaphoreType.DMA((n,)),
            ],
            compiler_params=pltpu.CompilerParams(
                collective_id=0, has_side_effects=True, vmem_limit_bytes=56 << 20),
        )(irrep_sizes, home, row_irrep, amplitudes, integrals)

    return jax.shard_map(
        body,
        mesh=mesh,
        in_specs=(P("aa", "grp", None), P(("grp", "aa"), None, None), P(), P(), P()),
        out_specs=P("grp", "aa"),
        check_vma=False,
    )
```

```python
import functools

import jax
import jax.numpy as jnp
from jax import lax
from jax.experimental import pallas as pl
from jax.experimental.pallas import tpu as pltpu
from jax.sharding import PartitionSpec as P

MESH = pl.DeviceIdType.MESH
UNROLL = 16


def each(first, last, step):
    if last - first <= UNROLL:
        for i in range(first, last):
            step(i)
    else:
        lax.fori_loop(first, last, lambda i, _: (step(i), 0)[1], 0)


def flipped(me, k, n):
    out, bit = me, 1
    while bit < n:
        mine = lax.rem(lax.div(me, bit), 2)
        flip = (k // bit) % 2
        out = out + flip * bit * (1 - 2 * mine)
        bit *= 2
    return out


def scan(count, step, init):
    chunk = 8 if count % 8 == 0 else 1

    def some(outer, state):
        for inner in range(chunk):
            state = step(outer * chunk + inner, state)
        return state

    return lax.fori_loop(0, count // chunk, some, init)


def kernel(n, most, sizes_in, home_in, row_irrep_in, amp, integ, out,
           sizes, home, row_irrep,
           amp_v, integ_v, send, recv, high, low, slot_of,
           index_sem, amp_sem, integ_sem, send_sem, recv_sem):
    me = lax.axis_index("aa")
    per = amp.shape[0]
    irreps, total = sizes.shape[0], home.shape[0]

    barrier = pltpu.get_barrier_semaphore()
    each(1, n, lambda k: pl.semaphore_signal(
        barrier, inc=1, device_id={"aa": flipped(me, k, n)}, device_id_type=MESH))
    get_index = [pltpu.make_async_copy(source, dest, index_sem.at[i]) for i, (source, dest) in enumerate(
        ((home_in, home), (sizes_in, sizes), (row_irrep_in, row_irrep)))]
    for copy in get_index:
        copy.start()
    get_amp = pltpu.make_async_copy(amp, amp_v, amp_sem)
    get_amp.start()
    get_integ = pltpu.make_async_copy(integ, integ_v, integ_sem)
    get_integ.start()

    for copy in get_index:
        copy.wait()
    offsets, at = [], jnp.int32(0)
    for g in range(irreps):
        offsets.append(at)
        at = at + sizes[g]

    def look(i, found):
        which = home[i] - me * per
        return tuple(jnp.where(which == q, i, found[q]) for q in range(per))

    places = scan(total, look, tuple(jnp.int32(0) for _ in range(per)))
    kinds = [sum((p >= offsets[g]).astype(jnp.int32) for g in range(1, irreps)) for p in places]

    get_amp.wait()

    def stage(k):
        dest = flipped(me, k, n)
        wanted = row_irrep[dest]
        pick = jnp.int32(0)
        has = jnp.bool_(False)
        for q in range(per):
            pick = jnp.where(kinds[q] == wanted, q, pick)
            has = has | (kinds[q] == wanted)
        block = amp_v[pick]
        send[dest] = jnp.where(has, block, 0.0)

    each(0, n, stage)

    def hop(k):
        peer = flipped(me, k, n)
        return pltpu.make_async_remote_copy(
            src_ref=send.at[peer], dst_ref=recv.at[me],
            send_sem=send_sem.at[peer], recv_sem=recv_sem.at[me],
            device_id={"aa": peer}, device_id_type=MESH)

    def landing(peer):
        return pltpu.make_async_remote_copy(
            src_ref=send.at[peer], dst_ref=recv.at[peer],
            send_sem=send_sem.at[peer], recv_sem=recv_sem.at[peer],
            device_id={"aa": peer}, device_id_type=MESH)

    pl.semaphore_wait(barrier, n - 1)
    each(0, n - 1, lambda i: hop(i + 1).start())

    mine = row_irrep[me]
    start = jnp.int32(0)
    count = jnp.int32(0)
    for g in range(irreps):
        start = jnp.where(mine == g, offsets[g], start)
        count = jnp.where(mine == g, sizes[g], count)

    def find(source):
        def look_at(m, found):
            row = home[jnp.minimum(start + m, total - 1)] - source * per
            return jnp.where((row >= 0) & (row < per) & (m < count), m, found)

        slot_of[source] = scan(most, look_at, jnp.int32(0))

    each(0, n, find)

    get_integ.wait()

    def split(m):
        full = integ_v[:, m, :].T
        top = full.astype(jnp.bfloat16)
        high[m] = top
        low[m] = (full - top.astype(jnp.float32)).astype(jnp.bfloat16)

    each(0, most, split)

    contract = (((1,), (0,)), ((), ()))

    def times(blocks, sources):
        full = jnp.concatenate(blocks, axis=1)
        top = full.astype(jnp.bfloat16)
        rest = (full - top.astype(jnp.float32)).astype(jnp.bfloat16)
        slots = [slot_of[s] for s in sources]
        upper = jnp.concatenate([high[m] for m in slots], axis=0)
        lower = jnp.concatenate([low[m] for m in slots], axis=0)
        both = lax.dot_general(jnp.concatenate([top, rest], axis=0), upper, contract,
                               preferred_element_type=jnp.float32)
        small = lax.dot_general(top, lower, contract, preferred_element_type=jnp.float32)
        half = top.shape[0]
        return both[:half] + (both[half:] + small)

    twin = flipped(me, 1, n)
    landing(twin).wait_recv()
    out[...] = times([send[me], recv[twin]], [me, twin])

    def pair(i):
        one, two = flipped(me, 2 * i, n), flipped(me, 2 * i + 1, n)
        landing(one).wait_recv()
        landing(two).wait_recv()
        out[...] += times([recv[one], recv[two]], [one, two])

    each(1, n // 2 - 1, pair)
    one, two = flipped(me, n - 2, n), flipped(me, n - 1, n)
    landing(one).wait_recv()
    landing(two).wait_recv()
    out[...] = 0.5 * (out[...] + times([recv[one], recv[two]], [one, two]))
    each(1, n, lambda k: hop(k).wait_send())


def solution(mesh):
    n = mesh.shape["aa"]

    def body(amplitudes, integrals, irrep_sizes, home, row_irrep):
        per, pairs, width = amplitudes.shape
        rows, most, _ = integrals.shape
        hbm = pl.BlockSpec(memory_space=pltpu.HBM)
        return pl.pallas_call(
            functools.partial(kernel, n, most),
            out_shape=pltpu.VMEM((pairs, rows), jnp.float32),
            in_specs=[hbm] * 5,
            out_specs=pl.BlockSpec(memory_space=pltpu.VMEM),
            scratch_shapes=[
                pltpu.SMEM(irrep_sizes.shape, jnp.int32),
                pltpu.SMEM(home.shape, jnp.int32),
                pltpu.SMEM(row_irrep.shape, jnp.int32),
                pltpu.VMEM((per, pairs, width), jnp.float32),
                pltpu.VMEM(integrals.shape, jnp.float32),
                pltpu.VMEM((n, pairs, width), jnp.float32),
                pltpu.VMEM((n, pairs, width), jnp.float32),
                pltpu.VMEM((most, width, rows), jnp.bfloat16),
                pltpu.VMEM((most, width, rows), jnp.bfloat16),
                pltpu.SMEM((n,), jnp.int32),
                pltpu.SemaphoreType.DMA((3,)),
                pltpu.SemaphoreType.DMA,
                pltpu.SemaphoreType.DMA,
                pltpu.SemaphoreType.DMA((n,)),
                pltpu.SemaphoreType.DMA((n,)),
            ],
            compiler_params=pltpu.CompilerParams(
                collective_id=0, has_side_effects=True, vmem_limit_bytes=56 << 20),
        )(irrep_sizes, home, row_irrep, amplitudes, integrals)

    return jax.shard_map(
        body,
        mesh=mesh,
        in_specs=(P("aa", "grp", None), P(("grp", "aa"), None, None), P(), P(), P()),
        out_specs=P("grp", "aa"),
        check_vma=False,
    )
```
